128 devices in a mesh: rows: 32 (over x, z, core), cols: 4 (over y).
Axes of the slice: x: 4, y: 4, z: 4, core: 2. Of those that a mesh axis runs over, the one named last changes fastest.
Arguments:
- gradient: bfloat16 [26624, 8192], P('rows', 'cols'), may hold values from -36 to 36
- momentum: float32 [26624, 8192], P('rows', 'cols'), may hold values from -6 to 6
- right_factor: float32 [8192, 512], P('cols'), may hold values from -0.0625 to 0.0625
Outputs:
- new_momentum: float32 [26624, 8192], P('rows', 'cols')
- new_factor: float32 [8192, 512], P('cols')
- left_basis: float32 [26624, 512], P('rows')
The draws below stay inside these ranges and needn't reach their ends.
All inputs are finite; a program needn't handle non-finite values.
Results may differ from the reference program's by a relative error of at most 0.0003.
Values sent between devices are 32-bit elements; how exact they have to be, the bound alone decides.
A program may use at most 128 MiB of HBM per device.

```python
import math
import jax
import jax.numpy as jnp
from jax import lax

ROWS = 26624
COLS = 8192
RANK = 512


def draw_gradient(key, part):
    key = jax.random.fold_in(key, 11)
    key_rows, key_cols, key_vals = jax.random.split(key, 3)
    row_scale = jnp.exp(jax.random.uniform(key_rows, (ROWS, 1), jnp.float32, math.log(0.3), math.log(3.0)))
    col_scale = jnp.exp(jax.random.uniform(key_cols, (1, COLS), jnp.float32, math.log(0.3), math.log(3.0)))
    entries = jnp.clip(jax.random.normal(key_vals, (ROWS, COLS), jnp.float32), -4.0, 4.0)
    return (entries * row_scale * col_scale).astype(jnp.bfloat16)


def block_levels(rng, extent, shards, smallest, top_value):
    level, own = 1.0, jax.random.fold_in(rng, 6)
    for position, blocks in shards:
        draws = jnp.exp(jax.random.uniform(jax.random.fold_in(own, position), (blocks,), jnp.float32, smallest / len(shards), top_value / len(shards)))
        level = level * jnp.repeat(draws, extent[position] // blocks).reshape([-1 if axis == position else 1 for axis in range(len(extent))])
    return level


def noise(rng, shape, width, most, cuts=(), kind=jnp.bfloat16):
    result = width * jax.random.normal(rng, shape, jnp.float32)
    if cuts:
        result = result * block_levels(rng, shape, cuts, -0.22, 0.18)
    return jnp.clip(result, -most, most).astype(kind)


def setup_inputs(seed: int = 0) -> dict:
    streams_of = jax.random.split(jax.random.key(seed), 4)
    return {
        "gradient": draw_gradient(jax.random.fold_in(streams_of[3], 71), 0),
        "momentum": noise(streams_of[1], (ROWS, COLS), 1.0, 6.0, ((0, 32), (1, 4)), jnp.float32),
        "right_factor": noise(streams_of[2], (COLS, RANK), COLS ** -0.5, 0.0625, ((0, 4),), jnp.float32),
    }


momentum_decay = 0.95
norm_eps = 1e-06

def exact_dot(left_arr, right_arr, dims):
    return lax.dot_general(left_arr.astype(jnp.float32), right_arr.astype(jnp.float32), (dims, ((), ())), precision=lax.Precision.HIGHEST, preferred_element_type=jnp.float32)

def reference(gradient, momentum, right_factor):
    blended = momentum + gradient.astype(jnp.float32)
    left = exact_dot(blended, right_factor, ((1,), (0,)))
    gram = exact_dot(left, left, ((0,), (0,)))
    lower_factor = jnp.linalg.cholesky(gram)
    inverse = lax.linalg.triangular_solve(lower_factor, jnp.eye(RANK, dtype=lower_factor.dtype), left_side=True, lower=True)
    left_basis = exact_dot(left, inverse, ((1,), (1,)))
    summed = exact_dot(blended, left_basis, ((0,), (0,)))
    col_squares = lax.optimization_barrier(jnp.sum(summed * summed, axis=0))
    new_factor = summed * lax.rsqrt(col_squares + norm_eps)
    new_momentum = blended - (1.0 - momentum_decay) * exact_dot(left_basis, summed, ((1,), (1,)))
    return (new_momentum, new_factor, left_basis)
```

```python
import jax
import jax.numpy as jnp
from jax import lax
from jax.experimental import pallas as pl
from jax.experimental.pallas import tpu as pltpu
from jax.sharding import PartitionSpec as P

momentum_decay = 0.95
norm_eps = 1e-06

F32 = jnp.float32
BF = jnp.bfloat16
M = 832
N = 2048
R = 512
YC = 208
BK = 128
NB = R // BK
TRI = [(i, j) for i in range(NB) for j in range(i, NB)]
GH = len(TRI) * BK // 2
GP = GH // 16
N_SEMS = 112


def split2(x):
    h = x.astype(BF)
    return h, (x - h.astype(F32)).astype(BF)


def split3(x):
    h = x.astype(BF)
    r = x - h.astype(F32)
    m = r.astype(BF)
    return h, m, (r - m.astype(F32)).astype(BF)


def dot(a, b, ca=1, cb=0):
    return lax.dot_general(a, b, (((ca,), (cb,)), ((), ())), preferred_element_type=F32)


def dot3(ah, al, bh, bl, ca=1, cb=0):
    return dot(ah, bh, ca, cb) + (dot(ah, bl, ca, cb) + dot(al, bh, ca, cb))


def prod6(a, b, ca, cb):
    ah, am, al = a
    bh, bm, bl = b
    lhs = jnp.concatenate([ah, ah, am, am, ah, al], axis=ca)
    rhs = jnp.concatenate([bh, bm, bh, bm, bl, bh], axis=cb)
    return dot(lhs, rhs, ca, cb)


def small_inverse(d_ref, tick, n=BK, b=16):
    row = lax.broadcasted_iota(jnp.int32, (b, n), 0)
    lane = lax.broadcasted_iota(jnp.int32, (b, n), 1)
    for s in range(n // b):
        r0 = s * b
        strip = d_ref[r0:r0 + b, :]
        cols = [jnp.broadcast_to(strip[:, r0 + j:r0 + j + 1], (b, n)) for j in range(b)]
        inside = (lane >= r0) & (lane < r0 + b)
        rows = jnp.where(inside, jnp.where(lane - r0 == row, 1.0, 0.0), strip)
        scale = jnp.zeros((b, n), F32)
        for j in range(b):
            pivot = jnp.broadcast_to(cols[j][j:j + 1], (b, n))
            scale = jnp.where(row == j, lax.rsqrt(pivot), scale)
            if j < b - 1:
                f = jnp.where(row > j, cols[j] * (1.0 / pivot), 0.0)
                for k in range(j + 1, b):
                    cols[k] = cols[k] - f * jnp.broadcast_to(cols[k][j:j + 1], (b, n))
                rows = rows - f * jnp.broadcast_to(rows[j:j + 1], (b, n))
        rows = rows * scale
        d_ref[r0:r0 + b, :] = rows
        if s < n // b - 1:
            sp = split3(rows)
            upd = prod6(sp, sp, 0, 0)
            t0 = r0 + b
            old = d_ref[t0:, :]
            lane2 = lax.broadcasted_iota(jnp.int32, old.shape, 1)
            old = jnp.where((lane2 >= r0) & (lane2 < t0), 0.0, old)
            d_ref[t0:, :] = old - upd[t0:, :]
        tick()


def chol_inverse(x_ref, d_ref, tick):
    ri = lax.broadcasted_iota(jnp.int32, (BK, BK), 0)
    ci = lax.broadcasted_iota(jnp.int32, (BK, BK), 1)
    for k in range(NB):
        k0 = k * BK
        d_ref[...] = x_ref[k0:k0 + BK, k0:k0 + BK]
        small_inverse(d_ref, tick)
        own = jnp.where(ci <= ri, d_ref[...], 0.0)
        own_split = split3(own)
        parts = []
        for j in range(NB):
            j0 = j * BK
            if j == k:
                parts.append(own)
            else:
                parts.append(prod6(own_split, split3(x_ref[k0:k0 + BK, j0:j0 + BK]), 1, 0))
            x_ref[k0:k0 + BK, j0:j0 + BK] = parts[j]
        sp = [split3(q) for q in parts]
        for i in range(k + 1, NB):
            for j in list(range(k + 1)) + list(range(i, NB)):
                u = prod6(sp[i], sp[j], 0, 0)
                i0, j0 = i * BK, j * BK
                if j == k:
                    x_ref[i0:i0 + BK, j0:j0 + BK] = -u
                else:
                    x_ref[i0:i0 + BK, j0:j0 + BK] = x_ref[i0:i0 + BK, j0:j0 + BK] - u


def mo(v, m=8):
    return pl.multiple_of(v, m)


class Copies:
    def __init__(self, send, recv):
        self.send, self.recv, self.n, self.all = send, recv, 0, []

    def start(self, src, dst, dev):
        i = self.n
        self.n += 1
        assert i < N_SEMS
        c = pltpu.make_async_remote_copy(
            src_ref=src, dst_ref=dst, send_sem=self.send.at[i], recv_sem=self.recv.at[i],
            device_id=dev, device_id_type=pl.DeviceIdType.MESH)
        c.start()
        self.all.append(c)
        return c

    def finish(self):
        for c in self.all:
            c.wait_send()


def add_into(dst, *srcs):
    t = dst[...]
    for s in srcs:
        t = t + s[...]
    dst[...] = t


class RingSum:
    def __init__(self, cp, half, buf, first, second, up, dn, a):
        self.cp, self.half, self.buf, self.up, self.dn = cp, half, buf, up, dn
        self.first, self.second = first, second
        self.me, self.u, self.d, self.o = a, lax.rem(a + 1, 4), lax.rem(a + 3, 4), lax.rem(a + 2, 4)

    def far(self):
        self.c1 = self.cp.start(self.half(self.buf, self.o, 0), self.first[0], self.up)
        self.c2 = self.cp.start(self.half(self.buf, self.o, 1), self.first[1], self.dn)

    def near_up(self):
        self.c3 = self.cp.start(self.half(self.buf, self.u, 1), self.half(self.second[0], 0, 1), self.up)

    def near_dn(self):
        self.c4 = self.cp.start(self.half(self.buf, self.d, 0), self.half(self.second[1], 0, 0), self.dn)

    def pass_up(self):
        self.c1.wait_recv()
        add_into(self.half(self.buf, self.u, 0), self.first[0])
        self.c5 = self.cp.start(self.half(self.buf, self.u, 0), self.half(self.second[0], 0, 0), self.up)

    def pass_dn(self):
        self.c2.wait_recv()
        add_into(self.half(self.buf, self.d, 1), self.first[1])
        self.c6 = self.cp.start(self.half(self.buf, self.d, 1), self.half(self.second[1], 0, 1), self.dn)

    def end(self, dst):
        self.c4.wait_recv()
        self.c5.wait_recv()
        self.c3.wait_recv()
        self.c6.wait_recv()
        for h in (0, 1):
            dst(h)[...] = (self.half(self.buf, self.me, h)[...] + self.half(self.second[0], 0, h)[...]) + self.half(self.second[1], 0, h)[...]


class RingGather:
    def __init__(self, cp, whole, half, buf, up, dn, a):
        self.cp, self.whole, self.half, self.buf, self.up, self.dn = cp, whole, half, buf, up, dn
        self.me, self.u, self.d = a, lax.rem(a + 1, 4), lax.rem(a + 3, 4)

    def start(self):
        w = self.whole(self.buf, self.me)
        self.c1 = self.cp.start(w, w, self.up)
        self.c2 = self.cp.start(w, w, self.dn)

    def forward(self):
        self.c1.wait_recv()
        h = self.half(self.buf, self.d, 0)
        self.c3 = self.cp.start(h, h, self.up)
        self.c2.wait_recv()
        h = self.half(self.buf, self.u, 1)
        self.c4 = self.cp.start(h, h, self.dn)

    def end(self):
        self.c3.wait_recv()
        self.c4.wait_recv()


def y_half(ref, c, h):
    return ref.at[pl.ds(mo(c * YC + h * (YC // 2)), YC // 2), :]


def y_whole(ref, c):
    return ref.at[pl.ds(mo(c * YC), YC), :]


def t1_half(ref, c, h):
    return ref.at[pl.ds(mo(c * 32 + h * 16), 16), :]


def t1_whole(ref, c):
    return ref.at[pl.ds(mo(c * 32), 32), :]


def t2_half(ref, c, h):
    return ref.at[pl.ds(mo(c * 8), 8), pl.ds(h * (N // 2), N // 2)]


def t2_whole(ref, c):
    return ref.at[pl.ds(mo(c * 8), 8), :]


def big_kernel(mom_hbm, grad_hbm, rf_hbm, st_ref, q_ref, scale_ref,
               mom, grad, rf, bh, bl, rfh, rfl, part, left, lth, ltl,
               y1u, y1d, y2u, y2d,
               gloc, gx, gsl, gmine, gys, gall, x_ref, d_ref,
               tt, tin, tacc, t1a, t1b, t2a, t2b, tmid, u1a, u1b, u2a, u2b, tall,
               sq_mine, sq_in, send, recv, load):
    rows, y = lax.axis_index("rows"), lax.axis_index("cols")
    core = lax.rem(rows, 2)
    chip = rows // 2
    z, x = lax.rem(chip, 4), chip // 4

    def dev(x_, z_, c_, y_):
        return ((x_ * 4 + z_) * 2 + c_, y_)

    def nxt(v, d):
        return lax.rem(v + d, 4)

    y_peer = {d: dev(x, z, core, nxt(y, d)) for d in (1, 2, 3)}
    x_peer = {d: dev(nxt(x, d), z, core, y) for d in (1, 2, 3)}
    z_peer = {d: dev(x, nxt(z, d), core, y) for d in (1, 2, 3)}
    sib = dev(x, z, 1 - core, y)
    plane = {d: (lax.rem(chip + d, 16) * 2 + core, y) for d in range(1, 16)}

    O, U, D = nxt(y, 2), nxt(y, 1), nxt(y, 3)
    order = [O, U, D, y]
    loads = [pltpu.make_async_copy(rf_hbm, rf, load.at[0])]
    for n, c in enumerate(order):
        loads.append(pltpu.make_async_copy(y_whole(mom_hbm, c), y_whole(mom, c), load.at[1 + 2 * n]))
        loads.append(pltpu.make_async_copy(y_whole(grad_hbm, c), y_whole(grad, c), load.at[2 + 2 * n]))
    for c in loads:
        c.start()

    barrier = pltpu.get_barrier_semaphore()
    peers = list(y_peer.values()) + list(plane.values()) + [sib]
    for p in peers:
        pl.semaphore_signal(barrier, inc=1, device_id=p, device_id_type=pl.DeviceIdType.MESH)

    cp = Copies(send, recv)
    loads[0].wait()
    h, l = split2(rf[...])
    rfh[...] = h
    rfl[...] = l

    def left_part(n):
        loads[1 + 2 * n].wait()
        loads[2 + 2 * n].wait()
        s = pl.ds(mo(order[n] * YC, 16), YC)
        h, l = split2(mom[s, :] + grad[s, :].astype(F32))
        bh[s, :] = h
        bl[s, :] = l
        part[s, :] = dot3(h, l, rfh[...], rfl[...])

    ring = RingSum(cp, y_half, part, (y1u, y1d), (y2u, y2d), y_peer[1], y_peer[3], y)
    left_part(0)
    pl.semaphore_wait(barrier, len(peers))
    ring.far()
    left_part(1)
    ring.near_up()
    left_part(2)
    ring.near_dn()
    left_part(3)
    ring.pass_up()
    ring.pass_dn()
    ring.end(lambda h: y_half(left, y, h))
    gather = RingGather(cp, y_whole, y_half, left, y_peer[1], y_peer[3], y)
    gather.start()

    sp = split3(y_whole(left, y)[...])
    for b, (i, j) in enumerate(TRI):
        g = prod6([s[:, i * BK:(i + 1) * BK] for s in sp], [s[:, j * BK:(j + 1) * BK] for s in sp], 0, 0)
        gloc[b * BK:(b + 1) * BK, :] = g
    c_core = cp.start(gloc.at[pl.ds(mo((1 - core) * GH), GH), :], gx, sib)

    def t_part(n, first=False):
        c = order[n]
        lt = jnp.transpose(y_whole(left, c)[...])
        h, l = split2(lt)
        lth[...] = h
        ltl[...] = l
        s = pl.ds(mo(c * YC, 16), YC)

        @pl.loop(0, N // 256)
        def _(n_):
            k = pl.ds(mo(n_ * 256, 256), 256)
            v = dot3(lth[...], ltl[...], bh[s, k], bl[s, k])
            if first:
                tt[:, k] = v
            else:
                tt[:, k] = tt[:, k] + v

    t_part(3, True)
    c_core.wait_recv()
    gh = pl.ds(mo(core * GH), GH)
    gx[...] = gx[...] + gloc[gh, :]

    def piece(ref, c):
        return ref.at[pl.ds(mo(c * GP), GP), :]

    cs = [cp.start(piece(gx, lax.rem(chip + d, 16)), gsl.at[d], plane[d]) for d in range(1, 16)]
    for c in cs:
        c.wait_recv()
    t = piece(gx, chip)[...]
    for d in range(1, 16):
        t = t + gsl[d]
    gmine[...] = t
    gys[y] = t
    cs = [cp.start(gmine, gys.at[y], y_peer[d]) for d in (1, 2, 3)]
    for c in cs:
        c.wait_recv()
    mine = piece(gall, core * 16 + chip)
    mine[...] = (gys[0] + gys[1]) + (gys[2] + gys[3])
    cs = [cp.start(mine, mine, plane[d]) for d in range(1, 16)]
    gather.forward()
    t_part(1)
    t_part(2)
    for c in cs:
        c.wait_recv()
    half = gall.at[gh, :]
    c_core = cp.start(half, half, sib)
    gather.end()
    t_part(0)
    c_core.wait_recv()
    for b, (i, j) in enumerate(TRI):
        x_ref[i * BK:(i + 1) * BK, j * BK:(j + 1) * BK] = gall[b * BK:(b + 1) * BK, :]

    def t_steps():
        up = [(x_peer[1], x_peer[3], x), (z_peer[1], z_peer[3], z)]
        c0 = []
        for p in (0, 1):
            c0.append(cp.start(tt.at[pl.ds(mo((1 - core) * 256 + p * 128), 128), :], tin.at[p], sib))
        yield
        r1 = []
        for p in (0, 1):
            c0[p].wait_recv()
            tacc[p] = tin[p] + tt[pl.ds(mo(core * 256 + p * 128), 128), :]
            r = RingSum(cp, t1_half, tacc.at[p], (t1a.at[p], t1b.at[p]), (t2a.at[p], t2b.at[p]), *up[p])
            r.far()
            r.near_up()
            r.near_dn()
            r1.append(r)
        yield
        for r in r1:
            r.pass_up()
            r.pass_dn()
        yield
        r2 = []
        for p in (0, 1):
            r1[p].end(lambda h: t1_half(tmid.at[p], 0, h))
            r = RingSum(cp, t2_half, tmid.at[p], (u1a.at[p], u1b.at[p]), (u2a.at[p], u2b.at[p]), *up[1 - p])
            r.far()
            r.near_up()
            r.near_dn()
            r2.append(r)
        yield
        for r in r2:
            r.pass_up()
            r.pass_dn()
        yield
        g2 = []
        for p in (0, 1):
            base = core * 256 + p * 128
            mid = tall.at[pl.ds(mo(base + up[p][2] * 32), 32), :]
            r2[p].end(lambda h: t2_half(mid, up[1 - p][2], h))
            g = RingGather(cp, t2_whole, t2_half, mid, *up[1 - p])
            g.start()
            g2.append(g)
        yield
        for g in g2:
            g.forward()
        yield
        g1 = []
        for p in (0, 1):
            g2[p].end()
            g = RingGather(cp, t1_whole, t1_half, tall.at[pl.ds(mo(core * 256 + p * 128), 128), :], *up[p])
            g.start()
            g1.append(g)
        yield
        for g in g1:
            g.forward()
        yield
        c1 = []
        for p in (0, 1):
            g1[p].end()
            h = tall.at[pl.ds(mo(core * 256 + p * 128), 128), :]
            c1.append(cp.start(h, h, sib))
        yield
        for c in c1:
            c.wait_recv()

    steps = t_steps()
    count = [0]
    when = {0: 0, 3: 1, 8: 2, 12: 3, 15: 4, 17: 5, 19: 6, 21: 7, 26: 8, 30: 9}

    def tick():
        if count[0] in when:
            next(steps, None)
        count[0] += 1

    tick()
    chol_inverse(x_ref, d_ref, tick)
    for _ in steps:
        pass

    vs = [split2(x_ref[i * BK:(i + 1) * BK, :(i + 1) * BK]) for i in range(NB)]

    @pl.loop(0, N // 256)
    def _(n_):
        k = pl.ds(mo(n_ * 256, 256), 256)
        th, tl = split2(tall[:, k])
        for i in range(NB):
            e = (i + 1) * BK
            v = dot3(vs[i][0], vs[i][1], th[:e], tl[:e])
            st_ref[i * BK:e, k] = v

    sq = jnp.zeros((R, 128), F32)
    for n_ in range(N // 128):
        v = st_ref[:, n_ * 128:(n_ + 1) * 128]
        sq = sq + v * v
    ones = jnp.ones((8, 128), BF)
    sh, sm, sl = split3(sq)
    sq_mine[...] = dot(ones, sh, 1, 1) + (dot(ones, sm, 1, 1) + dot(ones, sl, 1, 1))
    cs = [cp.start(sq_mine, sq_in.at[d], y_peer[d]) for d in (1, 2, 3)]
    lh, ll = split2(left[...])
    for j in range(NB):
        e = (j + 1) * BK
        q_ref[:, j * BK:e] = dot3(lh[:, :e], ll[:, :e], vs[j][0], vs[j][1], 1, 1)
    for c in cs:
        c.wait_recv()
    scale_ref[...] = lax.rsqrt(sq_mine[...] + sq_in[1] + sq_in[2] + sq_in[3] + norm_eps)
    cp.finish()


def last_kernel(mom_ref, grad_ref, q_ref, st_ref, scale_ref, nm_ref, nf_ref, lb_ref):
    @pl.when(pl.program_id(0) == 0)
    def _():
        lb_ref[...] = q_ref[...]

    st = st_ref[...]
    nm_ref[...] = (mom_ref[...] + grad_ref[...].astype(F32)) - (1.0 - momentum_decay) * dot(
        q_ref[...].astype(BF), st.astype(BF))
    nf_ref[...] = jnp.transpose(st) * scale_ref[0:1, :]


def body(gradient, momentum, right_factor):
    V = pltpu.VMEM
    big = pl.pallas_call(
        big_kernel,
        out_shape=(jax.ShapeDtypeStruct((R, N), F32), jax.ShapeDtypeStruct((M, R), F32),
                   jax.ShapeDtypeStruct((8, R), F32)),
        in_specs=[pl.BlockSpec(memory_space=pl.ANY)] * 3,
        out_specs=[pl.BlockSpec(memory_space=V)] * 3,
        scratch_shapes=[
            V((M, N), F32), V((M, N), BF), V((N, R), F32), V((M, N), BF), V((M, N), BF),
            V((N, R), BF), V((N, R), BF), V((M, R), F32), V((M, R), F32), V((R, YC), BF), V((R, YC), BF),
            V((YC // 2, R), F32), V((YC // 2, R), F32), V((YC, R), F32), V((YC, R), F32),
            V((2 * GH, BK), F32), V((GH, BK), F32), V((16, GP, BK), F32), V((GP, BK), F32), V((4, GP, BK), F32),
            V((2 * GH, BK), F32), V((R, R), F32), V((BK, BK), F32),
            V((R, N), F32), V((2, 128, N), F32), V((2, 128, N), F32),
            V((2, 16, N), F32), V((2, 16, N), F32), V((2, 32, N), F32), V((2, 32, N), F32), V((2, 32, N), F32),
            V((2, 8, N // 2), F32), V((2, 8, N // 2), F32), V((2, 8, N), F32), V((2, 8, N), F32), V((R, N), F32),
            V((8, R), F32), V((4, 8, R), F32),
            pltpu.SemaphoreType.DMA((N_SEMS,)), pltpu.SemaphoreType.DMA((N_SEMS,)), pltpu.SemaphoreType.DMA((9,)),
        ],
        compiler_params=pltpu.CompilerParams(
            collective_id=0, has_side_effects=True, vmem_limit_bytes=60 << 20),
        cost_estimate=pl.CostEstimate(flops=4 * M * N * R * 3, bytes_accessed=20 << 20, transcendentals=0),
    )
    st, q, scale = big(momentum, gradient, right_factor)
    tile = 256
    return pl.pallas_call(
        last_kernel,
        grid=(N // tile,),
        out_shape=(jax.ShapeDtypeStruct((M, N), F32), jax.ShapeDtypeStruct((N, R), F32),
                   jax.ShapeDtypeStruct((M, R), F32)),
        in_specs=[pl.BlockSpec((M, tile), lambda n: (0, n)), pl.BlockSpec((M, tile), lambda n: (0, n)),
                  pl.BlockSpec((M, R), lambda n: (0, 0)), pl.BlockSpec((R, tile), lambda n: (0, n)),
                  pl.BlockSpec((8, R), lambda n: (0, 0))],
        out_specs=[pl.BlockSpec((M, tile), lambda n: (0, n)), pl.BlockSpec((tile, R), lambda n: (n, 0)),
                   pl.BlockSpec((M, R), lambda n: (0, 0))],
        compiler_params=pltpu.CompilerParams(vmem_limit_bytes=40 << 20),
        cost_estimate=pl.CostEstimate(flops=2 * M * N * R, bytes_accessed=30 << 20, transcendentals=0),
    )(momentum, gradient, q, st, scale)


def solution(mesh):
    return jax.shard_map(
        body,
        mesh=mesh,
        in_specs=(P("rows", "cols"), P("rows", "cols"), P("cols", None)),
        out_specs=(P("rows", "cols"), P("cols", None), P("rows", None)),
        check_vma=False,
    )
```

```python
import jax
import jax.numpy as jnp
from jax import lax
from jax.experimental import pallas as pl
from jax.experimental.pallas import tpu as pltpu
from jax.sharding import PartitionSpec as P

momentum_decay = 0.95
norm_eps = 1e-06

F32 = jnp.float32
BF = jnp.bfloat16
M = 832
N = 2048
R = 512
YC = 208
BK = 128
NB = R // BK
TRI = [(i, j) for i in range(NB) for j in range(i, NB)]
GH = len(TRI) * BK // 2
GP = GH // 16
N_SEMS = 220


def split2(x):
    h = x.astype(BF)
    return h, (x - h.astype(F32)).astype(BF)


def split3(x):
    h = x.astype(BF)
    r = x - h.astype(F32)
    m = r.astype(BF)
    return h, m, (r - m.astype(F32)).astype(BF)


def dot(a, b, ca=1, cb=0):
    return lax.dot_general(a, b, (((ca,), (cb,)), ((), ())), preferred_element_type=F32)


def dot3(ah, al, bh, bl, ca=1, cb=0):
    return dot(ah, bh, ca, cb) + (dot(ah, bl, ca, cb) + dot(al, bh, ca, cb))


def prod6(a, b, ca, cb):
    ah, am, al = a
    bh, bm, bl = b
    lhs = jnp.concatenate([ah, ah, am, am, ah, al], axis=ca)
    rhs = jnp.concatenate([bh, bm, bh, bm, bl, bh], axis=cb)
    return dot(lhs, rhs, ca, cb)


def small_inverse(d_ref, tick, n=BK, b=16):
    row = lax.broadcasted_iota(jnp.int32, (b, n), 0)
    lane = lax.broadcasted_iota(jnp.int32, (b, n), 1)
    for s in range(n // b):
        r0 = s * b
        strip = d_ref[r0:r0 + b, :]
        cols = [jnp.broadcast_to(strip[:, r0 + j:r0 + j + 1], (b, n)) for j in range(b)]
        inside = (lane >= r0) & (lane < r0 + b)
        rows = jnp.where(inside, jnp.where(lane - r0 == row, 1.0, 0.0), strip)
        scale = jnp.zeros((b, n), F32)
        for j in range(b):
            pivot = jnp.broadcast_to(cols[j][j:j + 1], (b, n))
            scale = jnp.where(row == j, lax.rsqrt(pivot), scale)
            if j < b - 1:
                f = jnp.where(row > j, cols[j] * (1.0 / pivot), 0.0)
                for k in range(j + 1, b):
                    cols[k] = cols[k] - f * jnp.broadcast_to(cols[k][j:j + 1], (b, n))
                rows = rows - f * jnp.broadcast_to(rows[j:j + 1], (b, n))
        rows = rows * scale
        d_ref[r0:r0 + b, :] = rows
        if s < n // b - 1:
            sp = split3(rows)
            upd = prod6(sp, sp, 0, 0)
            t0 = r0 + b
            old = d_ref[t0:, :]
            lane2 = lax.broadcasted_iota(jnp.int32, old.shape, 1)
            old = jnp.where((lane2 >= r0) & (lane2 < t0), 0.0, old)
            d_ref[t0:, :] = old - upd[t0:, :]
        tick()


def chol_inverse(x_ref, d_ref, tick):
    ri = lax.broadcasted_iota(jnp.int32, (BK, BK), 0)
    ci = lax.broadcasted_iota(jnp.int32, (BK, BK), 1)
    for k in range(NB):
        k0 = k * BK
        d_ref[...] = x_ref[k0:k0 + BK, k0:k0 + BK]
        small_inverse(d_ref, tick)
        own = jnp.where(ci <= ri, d_ref[...], 0.0)
        own_split = split3(own)
        parts = []
        for j in range(NB):
            j0 = j * BK
            if j == k:
                parts.append(own)
            else:
                parts.append(prod6(own_split, split3(x_ref[k0:k0 + BK, j0:j0 + BK]), 1, 0))
            x_ref[k0:k0 + BK, j0:j0 + BK] = parts[j]
        sp = [split3(q) for q in parts]
        for i in range(k + 1, NB):
            for j in list(range(k + 1)) + list(range(i, NB)):
                u = prod6(sp[i], sp[j], 0, 0)
                i0, j0 = i * BK, j * BK
                if j == k:
                    x_ref[i0:i0 + BK, j0:j0 + BK] = -u
                else:
                    x_ref[i0:i0 + BK, j0:j0 + BK] = x_ref[i0:i0 + BK, j0:j0 + BK] - u


def mo(v, m=8):
    return pl.multiple_of(v, m)


class Copies:
    def __init__(self, send, recv):
        self.send, self.recv, self.n, self.all = send, recv, 0, []

    def start(self, src, dst, dev):
        i = self.n
        self.n += 1
        assert i < N_SEMS
        c = pltpu.make_async_remote_copy(
            src_ref=src, dst_ref=dst, send_sem=self.send.at[i], recv_sem=self.recv.at[i],
            device_id=dev, device_id_type=pl.DeviceIdType.MESH)
        c.start()
        self.all.append(c)
        return c

    def finish(self):
        for c in self.all:
            c.wait_send()
        self.all = []


def add_into(dst, *srcs):
    t = dst[...]
    for s in srcs:
        t = t + s[...]
    dst[...] = t


class RingSum:
    def __init__(self, cp, half, buf, first, second, up, dn, a):
        self.cp, self.half, self.buf, self.up, self.dn = cp, half, buf, up, dn
        self.first, self.second = first, second
        self.me, self.u, self.d, self.o = a, lax.rem(a + 1, 4), lax.rem(a + 3, 4), lax.rem(a + 2, 4)

    def far(self):
        self.c1 = self.cp.start(self.half(self.buf, self.o, 0), self.first[0], self.up)
        self.c2 = self.cp.start(self.half(self.buf, self.o, 1), self.first[1], self.dn)

    def near_up(self):
        self.c3 = self.cp.start(self.half(self.buf, self.u, 1), self.half(self.second[0], 0, 1), self.up)

    def near_dn(self):
        self.c4 = self.cp.start(self.half(self.buf, self.d, 0), self.half(self.second[1], 0, 0), self.dn)

    def pass_up(self):
        self.c1.wait_recv()
        add_into(self.half(self.buf, self.u, 0), self.first[0])
        self.c5 = self.cp.start(self.half(self.buf, self.u, 0), self.half(self.second[0], 0, 0), self.up)

    def pass_dn(self):
        self.c2.wait_recv()
        add_into(self.half(self.buf, self.d, 1), self.first[1])
        self.c6 = self.cp.start(self.half(self.buf, self.d, 1), self.half(self.second[1], 0, 1), self.dn)

    def end(self, dst):
        self.c4.wait_recv()
        self.c5.wait_recv()
        self.c3.wait_recv()
        self.c6.wait_recv()
        for h in (0, 1):
            dst(h)[...] = (self.half(self.buf, self.me, h)[...] + self.half(self.second[0], 0, h)[...]) + self.half(self.second[1], 0, h)[...]


class RingGather:
    def __init__(self, cp, whole, half, buf, up, dn, a):
        self.cp, self.whole, self.half, self.buf, self.up, self.dn = cp, whole, half, buf, up, dn
        self.me, self.u, self.d = a, lax.rem(a + 1, 4), lax.rem(a + 3, 4)

    def start(self):
        w = self.whole(self.buf, self.me)
        self.c1 = self.cp.start(w, w, self.up)
        self.c2 = self.cp.start(w, w, self.dn)

    def forward(self):
        self.c1.wait_recv()
        h = self.half(self.buf, self.d, 0)
        self.c3 = self.cp.start(h, h, self.up)
        self.c2.wait_recv()
        h = self.half(self.buf, self.u, 1)
        self.c4 = self.cp.start(h, h, self.dn)

    def end(self):
        self.c3.wait_recv()
        self.c4.wait_recv()


def y_half(ref, c, h):
    return ref.at[pl.ds(mo(c * YC + h * (YC // 2)), YC // 2), :]


def y_whole(ref, c):
    return ref.at[pl.ds(mo(c * YC), YC), :]


def t_half(ref, c, h):
    return ref.at[pl.ds(mo(c * 8), 8), pl.ds(h * (N // 2), N // 2)]


def t_whole(ref, c):
    return ref.at[pl.ds(mo(c * 8), 8), :]


def t_quarter(ref, c):
    return ref.at[:, pl.ds(mo(c * (N // 4), 128), N // 4)]


class GroupSum:
    def __init__(self, cp, g, core, ups, tt, tin, r1, r2, tmid, rq, tall, sib):
        self.cp, self.g, self.core, self.ups, self.sib = cp, g, core, ups, sib
        self.tt, self.tin, self.r1, self.r2, self.tmid, self.rq = tt, tin, r1, r2, tmid, rq
        self.tall = tall

    def pair(self):
        src = self.tt.at[pl.ds(mo(self.g * BK + (1 - self.core) * 64), 64), :]
        self.c0 = self.cp.start(src, self.tin.at[self.g], self.sib)

    def ring(self):
        self.c0.wait_recv()
        g = self.g
        own = self.tt.at[pl.ds(mo(g * BK + self.core * 64), 64), :]
        own[...] = self.tin[g] + own[...]
        self.rings = []
        for p in (0, 1):
            peer, a = self.ups[p]
            r = RingSum(self.cp, t_half, self.tt.at[pl.ds(mo(g * BK + self.core * 64 + 32 * p), 32), :],
                        (self.r1.at[g, p, 0], self.r1.at[g, p, 1]), (self.r2.at[g, p, 0], self.r2.at[g, p, 1]),
                        peer[1], peer[3], a)
            r.far()
            r.near_up()
            r.near_dn()
            self.rings.append(r)

    def ring_pass(self):
        for r in self.rings:
            r.pass_up()
            r.pass_dn()

    def direct(self):
        self.cq = []
        for p in (0, 1):
            mid = self.tmid.at[self.g, p]
            self.rings[p].end(lambda h: t_half(mid, 0, h))
            peer, a = self.ups[1 - p]
            for d in (1, 2, 3):
                self.cq.append(self.cp.start(t_quarter(mid, lax.rem(a + d, 4)), self.rq.at[self.g, p, d], peer[d]))

    def base(self, p):
        return self.tall.at[pl.ds(mo(self.g * BK + self.core * 64 + 32 * p), 32), :]

    def spread(self):
        for c in self.cq:
            c.wait_recv()
        self.cq = []
        for p in (0, 1):
            peer, a = self.ups[1 - p]
            rq = self.rq.at[self.g, p]
            out = t_quarter(t_whole(self.base(p), self.ups[p][1]), a)
            out[...] = (t_quarter(self.tmid.at[self.g, p], a)[...] + rq[1]) + (rq[2] + rq[3])
            for d in (1, 2, 3):
                self.cq.append(self.cp.start(out, out, peer[d]))

    def gather(self):
        for c in self.cq:
            c.wait_recv()
        self.gathers = []
        for p in (0, 1):
            peer, a = self.ups[p]
            r = RingGather(self.cp, t_whole, t_half, self.base(p), peer[1], peer[3], a)
            r.start()
            self.gathers.append(r)

    def gather_pass(self):
        for r in self.gathers:
            r.forward()

    def share(self):
        for r in self.gathers:
            r.end()
        h = self.tall.at[pl.ds(mo(self.g * BK + self.core * 64), 64), :]
        self.c1 = self.cp.start(h, h, self.sib)

    def done(self):
        self.c1.wait_recv()


def big_kernel(mom_hbm, grad_hbm, rf_hbm, st_hbm, q_hbm, scale_ref,
               mom, rf, bh, bl, rfh, rfl, part, left, ltc,
               y1u, y1d, y2u, y2d,
               gloc, gx, gsl, gmine, gys, gall, x_ref, d_ref,
               tin, r1, r2, tmid, rq, tall, st,
               sq_mine, sq_in, send, recv, load, rounds):
    rows, y = lax.axis_index("rows"), lax.axis_index("cols")
    core = lax.rem(rows, 2)
    chip = rows // 2
    z, x = lax.rem(chip, 4), chip // 4

    def dev(x_, z_, c_, y_):
        return ((x_ * 4 + z_) * 2 + c_, y_)

    def nxt(v, d):
        return lax.rem(v + d, 4)

    y_peer = {d: dev(x, z, core, nxt(y, d)) for d in (1, 2, 3)}
    x_peer = {d: dev(nxt(x, d), z, core, y) for d in (1, 2, 3)}
    z_peer = {d: dev(x, nxt(z, d), core, y) for d in (1, 2, 3)}
    sib = dev(x, z, 1 - core, y)
    plane = {d: (lax.rem(chip + d, 16) * 2 + core, y) for d in range(1, 16)}

    O, U, D = nxt(y, 2), nxt(y, 1), nxt(y, 3)
    order = [O, U, D, y]
    loads = [pltpu.make_async_copy(rf_hbm, rf, load.at[0])]
    for n, c in enumerate(order):
        loads.append(pltpu.make_async_copy(y_whole(mom_hbm, c), y_whole(mom, c), load.at[1 + 2 * n]))
        loads.append(pltpu.make_async_copy(y_whole(grad_hbm, c), y_whole(bh, c), load.at[2 + 2 * n]))
    for c in loads:
        c.start()

    barrier = pltpu.get_barrier_semaphore()
    near = [p[d] for p in (x_peer, y_peer, z_peer) for d in (1, 3)] + [sib]

    def greet(sem):
        for p in near:
            pl.semaphore_signal(sem, inc=1, device_id=p, device_id_type=pl.DeviceIdType.MESH)

    greet(barrier)

    cp = Copies(send, recv)
    loads[0].wait()
    h, l = split2(rf[...])
    rfh[...] = h
    rfl[...] = l

    def left_part(n):
        loads[1 + 2 * n].wait()
        loads[2 + 2 * n].wait()
        s = pl.ds(mo(order[n] * YC, 16), YC)
        h, l = split2(mom[s, :] + bh[s, :].astype(F32))
        bh[s, :] = h
        bl[s, :] = l
        v = dot3(h, l, rfh[...], rfl[...])
        for g in range(NB):
            part[g, s, :] = v[:, g * BK:(g + 1) * BK]

    rings = [RingSum(cp, y_half, part.at[g], (y1u.at[g], y1d.at[g]), (y2u.at[g], y2d.at[g]), y_peer[1], y_peer[3], y)
             for g in range(NB)]
    gathers = [RingGather(cp, y_whole, y_half, left.at[g], y_peer[1], y_peer[3], y) for g in range(NB)]
    left_part(0)
    pl.semaphore_wait(barrier, len(near))
    for r in rings:
        r.far()
    greet(rounds.at[0])
    left_part(1)
    for r in rings:
        r.near_up()
    left_part(2)
    for r in rings:
        r.near_dn()
    left_part(3)
    pl.semaphore_wait(rounds.at[0], len(near))
    greet(rounds.at[1])
    for r in rings:
        r.pass_up()
        r.pass_dn()
    pl.semaphore_wait(rounds.at[1], len(near))
    greet(rounds.at[2])
    own = pl.ds(mo(y * YC), YC)
    for g in range(NB):
        rings[g].end(lambda h: y_half(left.at[g], y, h))
        if g < 2:
            gathers[g].start()

    sp = [split3(left[g, own, :]) for g in range(NB)]
    for b, (i, j) in enumerate(TRI):
        gloc[b * BK:(b + 1) * BK, :] = prod6(sp[i], sp[j], 0, 0)
    c_core = cp.start(gloc.at[pl.ds(mo((1 - core) * GH), GH), :], gx, sib)

    tt = mom
    ups = [(x_peer, x), (z_peer, z)]
    sums = [GroupSum(cp, g, core, ups, tt, tin, r1, r2, tmid, rq, tall, sib) for g in range(NB)]

    def t_part(g):
        gathers[g].end()
        h, l = split2(jnp.transpose(left[g]))
        ltc[0:BK, :] = h
        ltc[BK:2 * BK, :] = l

        @pl.loop(0, N // 256)
        def _(n_):
            k = pl.ds(mo(n_ * 256, 256), 256)
            v = dot(ltc[...], bh[:, k])
            tt[g * BK:(g + 1) * BK, k] = v[:BK] + (v[BK:] + dot(ltc[0:BK, :], bl[:, k]))

        sums[g].pair()

    c_core.wait_recv()
    gh = pl.ds(mo(core * GH), GH)
    gx[...] = gx[...] + gloc[gh, :]

    def piece(ref, c):
        return ref.at[pl.ds(mo(c * GP), GP), :]

    pl.semaphore_wait(rounds.at[2], len(near))
    cs = [cp.start(piece(gx, lax.rem(chip + d, 16)), gsl.at[d], plane[d]) for d in range(1, 16)]
    gathers[0].forward()
    gathers[2].start()
    gathers[1].forward()
    gathers[3].start()
    t_part(0)
    for c in cs:
        c.wait_recv()
    t = piece(gx, chip)[...]
    for d in range(1, 16):
        t = t + gsl[d]
    gmine[...] = t
    gys[y] = t
    cs = [cp.start(gmine, gys.at[y], y_peer[d]) for d in (1, 2, 3)]
    gathers[2].forward()
    sums[0].ring()
    t_part(1)
    for c in cs:
        c.wait_recv()
    mine = piece(gall, core * 16 + chip)
    mine[...] = (gys[0] + gys[1]) + (gys[2] + gys[3])
    cs = [cp.start(mine, mine, plane[d]) for d in range(1, 16)]
    gathers[3].forward()
    t_part(2)
    sums[1].ring()
    sums[0].ring_pass()
    t_part(3)
    sums[2].ring()
    sums[1].ring_pass()
    for c in cs:
        c.wait_recv()
    half = gall.at[gh, :]
    c_core = cp.start(half, half, sib)
    sums[3].ring()
    sums[0].direct()
    c_core.wait_recv()
    for b, (i, j) in enumerate(TRI):
        x_ref[i * BK:(i + 1) * BK, j * BK:(j + 1) * BK] = gall[b * BK:(b + 1) * BK, :]

    s0, s1, s2, s3 = sums
    plan = {
        0: [s2.ring_pass, s1.direct], 2: [s0.spread], 4: [s3.ring_pass], 6: [s2.direct], 7: [s1.spread],
        9: [s0.gather], 10: [s3.direct], 13: [s2.spread], 14: [s1.gather], 16: [s0.gather_pass], 17: [s3.spread],
        20: [s2.gather], 21: [s1.gather_pass], 23: [s0.share], 24: [s3.gather], 26: [s2.gather_pass],
        27: [s1.share], 28: [s0.done], 30: [s3.gather_pass], 31: [s1.done], 32: [s2.share],
    }
    count = [0]

    def tick():
        for f in plan.get(count[0], ()):
            f()
        count[0] += 1

    tick()
    chol_inverse(x_ref, d_ref, tick)
    for n_ in range(count[0], 40):
        tick()

    vs = [split2(x_ref[i * BK:(i + 1) * BK, :(i + 1) * BK]) for i in range(NB)]
    lh, ll = split2(jnp.concatenate([left[g] for g in range(NB)], axis=1))
    q_buf = rf.at[0:M, :]
    for j in range(NB):
        e = (j + 1) * BK
        q_buf[:, j * BK:e] = dot3(lh[:, :e], ll[:, :e], vs[j][0], vs[j][1], 1, 1)
    out_q = pltpu.make_async_copy(q_buf, q_hbm, load.at[0])
    out_q.start()
    ones = jnp.ones((8, BK), BF)
    outs = []

    def summed(i):
        e = (i + 1) * BK
        sq = jnp.zeros((BK, BK), F32)
        for n_ in range(N // 512):
            k = pl.ds(n_ * 512, 512)
            th, tl = split2(tall[:e, k])
            v = dot3(vs[i][0], vs[i][1], th, tl)
            st[i * BK:e, k] = v
            for m_ in range(4):
                w = v[:, m_ * BK:(m_ + 1) * BK]
                sq = sq + w * w
        sh, sm, sl = split3(sq)
        sq_mine[:, i * BK:e] = dot(ones, sh, 1, 1) + (dot(ones, sm, 1, 1) + dot(ones, sl, 1, 1))
        c = pltpu.make_async_copy(st.at[i * BK:e, :], st_hbm.at[i * BK:e, :], load.at[1 + i])
        c.start()
        outs.append(c)

    summed(0)
    s3.share()
    summed(1)
    s2.done()
    summed(2)
    s3.done()
    summed(3)
    cs = [cp.start(sq_mine, sq_in.at[d], y_peer[d]) for d in (1, 2, 3)]
    cp.finish()
    for c in [out_q] + outs:
        c.wait()
    for c in cs:
        c.wait_recv()
    scale_ref[...] = lax.rsqrt(sq_mine[...] + sq_in[1] + sq_in[2] + sq_in[3] + norm_eps)
    cp.finish()


def last_kernel(mom_ref, grad_ref, q_ref, st_ref, scale_ref, nm_ref, nf_ref, lb_ref):
    @pl.when(pl.program_id(0) == 0)
    def _():
        lb_ref[...] = q_ref[...]

    st = st_ref[...]
    nm_ref[...] = (mom_ref[...] + grad_ref[...].astype(F32)) - (1.0 - momentum_decay) * dot(
        q_ref[...].astype(BF), st.astype(BF))
    nf_ref[...] = jnp.transpose(st) * scale_ref[0:1, :]


def body(gradient, momentum, right_factor):
    V = pltpu.VMEM
    big = pl.pallas_call(
        big_kernel,
        out_shape=(jax.ShapeDtypeStruct((R, N), F32), jax.ShapeDtypeStruct((M, R), F32),
                   jax.ShapeDtypeStruct((8, R), F32)),
        in_specs=[pl.BlockSpec(memory_space=pltpu.HBM)] * 3,
        out_specs=[pl.BlockSpec(memory_space=pl.ANY)] * 2 + [pl.BlockSpec(memory_space=V)],
        scratch_shapes=[
            V((M, N), F32), V((N, R), F32), V((M, N), BF), V((M, N), BF),
            V((N, R), BF), V((N, R), BF), V((NB, M, BK), F32), V((NB, M, BK), F32), V((2 * BK, M), BF),
            V((NB, YC // 2, BK), F32), V((NB, YC // 2, BK), F32), V((NB, YC, BK), F32), V((NB, YC, BK), F32),
            V((2 * GH, BK), F32), V((GH, BK), F32), V((16, GP, BK), F32), V((GP, BK), F32), V((4, GP, BK), F32),
            V((2 * GH, BK), F32), V((R, R), F32), V((BK, BK), F32),
            V((NB, 64, N), F32),
            V((NB, 2, 2, 8, N // 2), F32), V((NB, 2, 2, 8, N), F32), V((NB, 2, 8, N), F32),
            V((NB, 2, 4, 8, N // 4), F32), V((R, N), F32), V((R, N), F32),
            V((8, R), F32), V((4, 8, R), F32),
            pltpu.SemaphoreType.DMA((N_SEMS,)), pltpu.SemaphoreType.DMA((N_SEMS,)), pltpu.SemaphoreType.DMA((9,)), pltpu.SemaphoreType.REGULAR((3,)),
        ],
        compiler_params=pltpu.CompilerParams(
            collective_id=0, has_side_effects=True, vmem_limit_bytes=50 << 20),
        cost_estimate=pl.CostEstimate(flops=4 * M * N * R * 3, bytes_accessed=20 << 20, transcendentals=0),
    )
    st, q, scale = big(momentum, gradient, right_factor)
    tile = 256
    return pl.pallas_call(
        last_kernel,
        grid=(N // tile,),
        out_shape=(jax.ShapeDtypeStruct((M, N), F32), jax.ShapeDtypeStruct((N, R), F32),
                   jax.ShapeDtypeStruct((M, R), F32)),
        in_specs=[pl.BlockSpec((M, tile), lambda n: (0, n)), pl.BlockSpec((M, tile), lambda n: (0, n)),
                  pl.BlockSpec((M, R), lambda n: (0, 0)), pl.BlockSpec((R, tile), lambda n: (0, n)),
                  pl.BlockSpec((8, R), lambda n: (0, 0))],
        out_specs=[pl.BlockSpec((M, tile), lambda n: (0, n)), pl.BlockSpec((tile, R), lambda n: (n, 0)),
                   pl.BlockSpec((M, R), lambda n: (0, 0))],
        compiler_params=pltpu.CompilerParams(vmem_limit_bytes=24 << 20),
        cost_estimate=pl.CostEstimate(flops=2 * M * N * R, bytes_accessed=30 << 20, transcendentals=0),
    )(momentum, gradient, q, st, scale)


def solution(mesh):
    return jax.shard_map(
        body,
        mesh=mesh,
        in_specs=(P("rows", "cols"), P("rows", "cols"), P("cols", None)),
        out_specs=(P("rows", "cols"), P("cols", None), P("rows", None)),
        check_vma=False,
    )
```

```python
import jax
import jax.numpy as jnp
from jax import lax
from jax.experimental import pallas as pl
from jax.experimental.pallas import tpu as pltpu
from jax.sharding import PartitionSpec as P

momentum_decay = 0.95
norm_eps = 1e-06

F32 = jnp.float32
BF = jnp.bfloat16
M = 832
N = 2048
R = 512
YC = 208
BK = 128
NB = R // BK
TRI = [(i, j) for i in range(NB) for j in range(i, NB)]
GH = len(TRI) * BK // 2
GP = GH // 16
N_SEMS = 220


def split2(x):
    h = x.astype(BF)
    return h, (x - h.astype(F32)).astype(BF)


def split3(x):
    h = x.astype(BF)
    r = x - h.astype(F32)
    m = r.astype(BF)
    return h, m, (r - m.astype(F32)).astype(BF)


def dot(a, b, ca=1, cb=0):
    return lax.dot_general(a, b, (((ca,), (cb,)), ((), ())), preferred_element_type=F32)


def dot3(ah, al, bh, bl, ca=1, cb=0):
    return dot(ah, bh, ca, cb) + (dot(ah, bl, ca, cb) + dot(al, bh, ca, cb))


def prod6(a, b, ca, cb):
    ah, am, al = a
    bh, bm, bl = b
    lhs = jnp.concatenate([ah, ah, am, am, ah, al], axis=ca)
    rhs = jnp.concatenate([bh, bm, bh, bm, bl, bh], axis=cb)
    return dot(lhs, rhs, ca, cb)


def small_inverse(d_ref, tick, n=BK, b=16):
    row = lax.broadcasted_iota(jnp.int32, (b, n), 0)
    lane = lax.broadcasted_iota(jnp.int32, (b, n), 1)
    for s in range(n // b):
        r0 = s * b
        strip = d_ref[r0:r0 + b, :]
        cols = [jnp.broadcast_to(strip[:, r0 + j:r0 + j + 1], (b, n)) for j in range(b)]
        inside = (lane >= r0) & (lane < r0 + b)
        rows = jnp.where(inside, jnp.where(lane - r0 == row, 1.0, 0.0), strip)
        scale = jnp.zeros((b, n), F32)
        for j in range(b):
            pivot = jnp.broadcast_to(cols[j][j:j + 1], (b, n))
            scale = jnp.where(row == j, lax.rsqrt(pivot), scale)
            if j < b - 1:
                f = jnp.where(row > j, cols[j] * (1.0 / pivot), 0.0)
                for k in range(j + 1, b):
                    cols[k] = cols[k] - f * jnp.broadcast_to(cols[k][j:j + 1], (b, n))
                rows = rows - f * jnp.broadcast_to(rows[j:j + 1], (b, n))
        rows = rows * scale
        d_ref[r0:r0 + b, :] = rows
        if s < n // b - 1:
            sp = split3(rows)
            upd = prod6(sp, sp, 0, 0)
            t0 = r0 + b
            old = d_ref[t0:, :]
            lane2 = lax.broadcasted_iota(jnp.int32, old.shape, 1)
            old = jnp.where((lane2 >= r0) & (lane2 < t0), 0.0, old)
            d_ref[t0:, :] = old - upd[t0:, :]
        tick()


def chol_inverse(x_ref, d_ref, tick):
    ri = lax.broadcasted_iota(jnp.int32, (BK, BK), 0)
    ci = lax.broadcasted_iota(jnp.int32, (BK, BK), 1)
    for k in range(NB):
        k0 = k * BK
        d_ref[...] = x_ref[k0:k0 + BK, k0:k0 + BK]
        small_inverse(d_ref, tick)
        own = jnp.where(ci <= ri, d_ref[...], 0.0)
        own_split = split3(own)
        parts = []
        for j in range(NB):
            j0 = j * BK
            if j == k:
                parts.append(own)
            else:
                parts.append(prod6(own_split, split3(x_ref[k0:k0 + BK, j0:j0 + BK]), 1, 0))
            x_ref[k0:k0 + BK, j0:j0 + BK] = parts[j]
        sp = [split3(q) for q in parts]
        for i in range(k + 1, NB):
            for j in list(range(k + 1)) + list(range(i, NB)):
                u = prod6(sp[i], sp[j], 0, 0)
                i0, j0 = i * BK, j * BK
                if j == k:
                    x_ref[i0:i0 + BK, j0:j0 + BK] = -u
                else:
                    x_ref[i0:i0 + BK, j0:j0 + BK] = x_ref[i0:i0 + BK, j0:j0 + BK] - u


def mo(v, m=8):
    return pl.multiple_of(v, m)


class Copies:
    def __init__(self, send, recv):
        self.send, self.recv, self.n, self.all = send, recv, 0, []

    def start(self, src, dst, dev):
        i = self.n
        self.n += 1
        assert i < N_SEMS
        c = pltpu.make_async_remote_copy(
            src_ref=src, dst_ref=dst, send_sem=self.send.at[i], recv_sem=self.recv.at[i],
            device_id=dev, device_id_type=pl.DeviceIdType.MESH)
        c.start()
        self.all.append(c)
        return c

    def finish(self):
        for c in self.all:
            c.wait_send()
        self.all = []


def add_into(dst, *srcs):
    t = dst[...]
    for s in srcs:
        t = t + s[...]
    dst[...] = t


class RingSum:
    def __init__(self, cp, half, buf, first, second, up, dn, a):
        self.cp, self.half, self.buf, self.up, self.dn = cp, half, buf, up, dn
        self.first, self.second = first, second
        self.me, self.u, self.d, self.o = a, lax.rem(a + 1, 4), lax.rem(a + 3, 4), lax.rem(a + 2, 4)

    def far(self):
        self.c1 = self.cp.start(self.half(self.buf, self.o, 0), self.first[0], self.up)
        self.c2 = self.cp.start(self.half(self.buf, self.o, 1), self.first[1], self.dn)

    def near_up(self):
        self.c3 = self.cp.start(self.half(self.buf, self.u, 1), self.half(self.second[0], 0, 1), self.up)

    def near_dn(self):
        self.c4 = self.cp.start(self.half(self.buf, self.d, 0), self.half(self.second[1], 0, 0), self.dn)

    def pass_up(self):
        self.c1.wait_recv()
        add_into(self.half(self.buf, self.u, 0), self.first[0])
        self.c5 = self.cp.start(self.half(self.buf, self.u, 0), self.half(self.second[0], 0, 0), self.up)

    def pass_dn(self):
        self.c2.wait_recv()
        add_into(self.half(self.buf, self.d, 1), self.first[1])
        self.c6 = self.cp.start(self.half(self.buf, self.d, 1), self.half(self.second[1], 0, 1), self.dn)

    def end(self, dst):
        self.c4.wait_recv()
        self.c5.wait_recv()
        self.c3.wait_recv()
        self.c6.wait_recv()
        for h in (0, 1):
            dst(h)[...] = (self.half(self.buf, self.me, h)[...] + self.half(self.second[0], 0, h)[...]) + self.half(self.second[1], 0, h)[...]


class RingGather:
    def __init__(self, cp, whole, half, buf, up, dn, a):
        self.cp, self.whole, self.half, self.buf, self.up, self.dn = cp, whole, half, buf, up, dn
        self.me, self.u, self.d = a, lax.rem(a + 1, 4), lax.rem(a + 3, 4)

    def start(self):
        w = self.whole(self.buf, self.me)
        self.c1 = self.cp.start(w, w, self.up)
        self.c2 = self.cp.start(w, w, self.dn)

    def forward(self):
        self.c1.wait_recv()
        h = self.half(self.buf, self.d, 0)
        self.c3 = self.cp.start(h, h, self.up)
        self.c2.wait_recv()
        h = self.half(self.buf, self.u, 1)
        self.c4 = self.cp.start(h, h, self.dn)

    def end(self):
        self.c3.wait_recv()
        self.c4.wait_recv()


def y_half(ref, c, h):
    return ref.at[pl.ds(mo(c * YC + h * (YC // 2)), YC // 2), :]


def y_whole(ref, c):
    return ref.at[pl.ds(mo(c * YC), YC), :]


def t_half(ref, c, h):
    return ref.at[pl.ds(mo(c * 8), 8), pl.ds(h * (N // 2), N // 2)]


def t_whole(ref, c):
    return ref.at[pl.ds(mo(c * 8), 8), :]


def t_quarter(ref, c):
    return ref.at[:, pl.ds(mo(c * (N // 4), 128), N // 4)]


class GroupSum:
    def __init__(self, cp, g, core, ups, tt, tin, r1, r2, tmid, rq, tall, sib):
        self.cp, self.g, self.core, self.ups, self.sib = cp, g, core, ups, sib
        self.tt, self.tin, self.r1, self.r2, self.tmid, self.rq = tt, tin, r1, r2, tmid, rq
        self.tall = tall

    def pair(self):
        src = self.tt.at[pl.ds(mo(self.g * BK + (1 - self.core) * 64), 64), :]
        self.c0 = self.cp.start(src, self.tin.at[self.g], self.sib)

    def ring(self):
        self.c0.wait_recv()
        g = self.g
        own = self.tt.at[pl.ds(mo(g * BK + self.core * 64), 64), :]
        own[...] = self.tin[g] + own[...]
        self.rings = []
        for p in (0, 1):
            peer, a = self.ups[p]
            r = RingSum(self.cp, t_half, self.tt.at[pl.ds(mo(g * BK + self.core * 64 + 32 * p), 32), :],
                        (self.r1.at[g, p, 0], self.r1.at[g, p, 1]), (self.r2.at[g, p, 0], self.r2.at[g, p, 1]),
                        peer[1], peer[3], a)
            r.far()
            r.near_up()
            r.near_dn()
            self.rings.append(r)

    def ring_pass(self):
        for r in self.rings:
            r.pass_up()
            r.pass_dn()

    def direct(self):
        self.cq = []
        for p in (0, 1):
            mid = self.tmid.at[self.g, p]
            self.rings[p].end(lambda h: t_half(mid, 0, h))
            peer, a = self.ups[1 - p]
            for d in (1, 2, 3):
                self.cq.append(self.cp.start(t_quarter(mid, lax.rem(a + d, 4)), self.rq.at[self.g, p, d], peer[d]))

    def base(self, p):
        return self.tall.at[pl.ds(mo(self.g * BK + self.core * 64 + 32 * p), 32), :]

    def spread(self):
        for c in self.cq:
            c.wait_recv()
        self.cq = []
        for p in (0, 1):
            peer, a = self.ups[1 - p]
            rq = self.rq.at[self.g, p]
            out = t_quarter(t_whole(self.base(p), self.ups[p][1]), a)
            out[...] = (t_quarter(self.tmid.at[self.g, p], a)[...] + rq[1]) + (rq[2] + rq[3])
            for d in (1, 2, 3):
                self.cq.append(self.cp.start(out, out, peer[d]))

    def gather(self):
        for c in self.cq:
            c.wait_recv()
        self.gathers = []
        for p in (0, 1):
            peer, a = self.ups[p]
            r = RingGather(self.cp, t_whole, t_half, self.base(p), peer[1], peer[3], a)
            r.start()
            self.gathers.append(r)

    def gather_pass(self):
        for r in self.gathers:
            r.forward()

    def share(self):
        for r in self.gathers:
            r.end()
        h = self.tall.at[pl.ds(mo(self.g * BK + self.core * 64), 64), :]
        self.c1 = self.cp.start(h, h, self.sib)

    def done(self):
        self.c1.wait_recv()


def big_kernel(mom_hbm, grad_hbm, rf_hbm, st_hbm, q_hbm, scale_ref,
               mom, rf, bh, bl, rfh, rfl, part, left, ltc,
               y1u, y1d, y2u, y2d,
               gloc, gx, gsl, gmine, gys, gall, x_ref, d_ref,
               tin, r1, r2, tmid, rq, tall, st,
               sq_mine, sq_in, send, recv, load, rounds):
    rows, y = lax.axis_index("rows"), lax.axis_index("cols")
    core = lax.rem(rows, 2)
    chip = rows // 2
    z, x = lax.rem(chip, 4), chip // 4

    def dev(x_, z_, c_, y_):
        return ((x_ * 4 + z_) * 2 + c_, y_)

    def nxt(v, d):
        return lax.rem(v + d, 4)

    y_peer = {d: dev(x, z, core, nxt(y, d)) for d in (1, 2, 3)}
    x_peer = {d: dev(nxt(x, d), z, core, y) for d in (1, 2, 3)}
    z_peer = {d: dev(x, nxt(z, d), core, y) for d in (1, 2, 3)}
    sib = dev(x, z, 1 - core, y)
    plane = {d: (lax.rem(chip + d, 16) * 2 + core, y) for d in range(1, 16)}

    O, U, D = nxt(y, 2), nxt(y, 1), nxt(y, 3)
    order = [O, U, D, y]
    loads = [pltpu.make_async_copy(rf_hbm, rf, load.at[0])]
    for n, c in enumerate(order):
        loads.append(pltpu.make_async_copy(y_whole(mom_hbm, c), y_whole(mom, c), load.at[1 + 2 * n]))
        loads.append(pltpu.make_async_copy(y_whole(grad_hbm, c), y_whole(bh, c), load.at[2 + 2 * n]))
    for c in loads:
        c.start()

    barrier = pltpu.get_barrier_semaphore()
    near = [p[d] for p in (x_peer, y_peer, z_peer) for d in (1, 3)] + [sib]

    def greet(sem):
        for p in near:
            pl.semaphore_signal(sem, inc=1, device_id=p, device_id_type=pl.DeviceIdType.MESH)

    greet(barrier)

    cp = Copies(send, recv)
    loads[0].wait()
    h, l = split2(rf[...])
    rfh[...] = h
    rfl[...] = l

    def left_part(n):
        loads[1 + 2 * n].wait()
        loads[2 + 2 * n].wait()
        s = pl.ds(mo(order[n] * YC, 16), YC)
        h, l = split2(mom[s, :] + bh[s, :].astype(F32))
        bh[s, :] = h
        bl[s, :] = l
        v = dot3(h, l, rfh[...], rfl[...])
        for g in range(NB):
            part[g, s, :] = v[:, g * BK:(g + 1) * BK]

    rings = [RingSum(cp, y_half, part.at[g], (y1u.at[g], y1d.at[g]), (y2u.at[g], y2d.at[g]), y_peer[1], y_peer[3], y)
             for g in range(NB)]
    gathers = [RingGather(cp, y_whole, y_half, left.at[g], y_peer[1], y_peer[3], y) for g in range(NB)]
    left_part(0)
    pl.semaphore_wait(barrier, len(near))
    for r in rings:
        r.far()
    greet(rounds.at[0])
    left_part(1)
    for r in rings:
        r.near_up()
    left_part(2)
    for r in rings:
        r.near_dn()
    left_part(3)
    pl.semaphore_wait(rounds.at[0], len(near))
    greet(rounds.at[1])
    for r in rings:
        r.pass_up()
        r.pass_dn()
    pl.semaphore_wait(rounds.at[1], len(near))
    greet(rounds.at[2])
    own = pl.ds(mo(y * YC), YC)
    for g in range(NB):
        rings[g].end(lambda h: y_half(left.at[g], y, h))
        if g < 2:
            gathers[g].start()

    sp = [split3(left[g, own, :]) for g in range(NB)]
    for b, (i, j) in enumerate(TRI):
        gloc[b * BK:(b + 1) * BK, :] = prod6(sp[i], sp[j], 0, 0)
    c_core = cp.start(gloc.at[pl.ds(mo((1 - core) * GH), GH), :], gx, sib)

    tt = mom
    ups = [(x_peer, x), (z_peer, z)]
    sums = [GroupSum(cp, g, core, ups, tt, tin, r1, r2, tmid, rq, tall, sib) for g in range(NB)]

    def t_part(g):
        gathers[g].end()
        h, l = split2(jnp.transpose(left[g]))
        ltc[0:BK, :] = h
        ltc[BK:2 * BK, :] = l

        for n_ in range(N // 1024):
            k = pl.ds(n_ * 1024, 1024)
            v = dot(ltc[...], bh[:, k])
            tt[g * BK:(g + 1) * BK, k] = v[:BK] + (v[BK:] + dot(ltc[0:BK, :], bl[:, k]))

        sums[g].pair()

    c_core.wait_recv()
    gh = pl.ds(mo(core * GH), GH)
    gx[...] = gx[...] + gloc[gh, :]

    def piece(ref, c):
        return ref.at[pl.ds(mo(c * GP), GP), :]

    pl.semaphore_wait(rounds.at[2], len(near))
    cs = [cp.start(piece(gx, lax.rem(chip + d, 16)), gsl.at[d], plane[d]) for d in range(1, 16)]
    gathers[0].forward()
    gathers[2].start()
    gathers[1].forward()
    gathers[3].start()
    t_part(0)
    for c in cs:
        c.wait_recv()
    t = piece(gx, chip)[...]
    for d in range(1, 16):
        t = t + gsl[d]
    gmine[...] = t
    gys[y] = t
    cs = [cp.start(gmine, gys.at[y], y_peer[d]) for d in (1, 2, 3)]
    gathers[2].forward()
    sums[0].ring()
    t_part(1)
    for c in cs:
        c.wait_recv()
    mine = piece(gall, core * 16 + chip)
    mine[...] = (gys[0] + gys[1]) + (gys[2] + gys[3])
    cs = [cp.start(mine, mine, plane[d]) for d in range(1, 16)]
    gathers[3].forward()
    t_part(2)
    sums[1].ring()
    sums[0].ring_pass()
    t_part(3)
    sums[2].ring()
    sums[1].ring_pass()
    for c in cs:
        c.wait_recv()
    half = gall.at[gh, :]
    c_core = cp.start(half, half, sib)
    sums[3].ring()
    sums[0].direct()
    c_core.wait_recv()
    for b, (i, j) in enumerate(TRI):
        x_ref[i * BK:(i + 1) * BK, j * BK:(j + 1) * BK] = gall[b * BK:(b + 1) * BK, :]

    s0, s1, s2, s3 = sums
    plan = {
        0: [s2.ring_pass, s1.direct], 2: [s0.spread], 4: [s3.ring_pass], 6: [s2.direct], 7: [s1.spread],
        9: [s0.gather], 10: [s3.direct], 13: [s2.spread], 14: [s1.gather], 16: [s0.gather_pass], 17: [s3.spread],
        20: [s2.gather], 21: [s1.gather_pass], 23: [s0.share], 24: [s3.gather], 26: [s2.gather_pass],
        27: [s1.share], 28: [s0.done], 30: [s3.gather_pass], 31: [s1.done], 32: [s2.share],
    }
    count = [0]

    def tick():
        for f in plan.get(count[0], ()):
            f()
        count[0] += 1

    tick()
    chol_inverse(x_ref, d_ref, tick)
    for n_ in range(count[0], 40):
        tick()

    vs = [split2(x_ref[i * BK:(i + 1) * BK, :(i + 1) * BK]) for i in range(NB)]
    lh, ll = split2(jnp.concatenate([left[g] for g in range(NB)], axis=1))
    q_buf = rf.at[0:M, :]
    for j in range(NB):
        e = (j + 1) * BK
        q_buf[:, j * BK:e] = dot3(lh[:, :e], ll[:, :e], vs[j][0], vs[j][1], 1, 1)
    out_q = pltpu.make_async_copy(q_buf, q_hbm, load.at[0])
    out_q.start()
    ones = jnp.ones((8, BK), BF)
    outs = []

    def summed(i):
        e = (i + 1) * BK
        sq = jnp.zeros((BK, BK), F32)
        for n_ in range(N // 512):
            k = pl.ds(n_ * 512, 512)
            th, tl = split2(tall[:e, k])
            v = dot3(vs[i][0], vs[i][1], th, tl)
            st[i * BK:e, k] = v
            for m_ in range(4):
                w = v[:, m_ * BK:(m_ + 1) * BK]
                sq = sq + w * w
        sh, sm, sl = split3(sq)
        sq_mine[:, i * BK:e] = dot(ones, sh, 1, 1) + (dot(ones, sm, 1, 1) + dot(ones, sl, 1, 1))
        c = pltpu.make_async_copy(st.at[i * BK:e, :], st_hbm.at[i * BK:e, :], load.at[1 + i])
        c.start()
        outs.append(c)

    summed(0)
    s3.share()
    summed(1)
    s2.done()
    summed(2)
    s3.done()
    summed(3)
    cs = [cp.start(sq_mine, sq_in.at[d], y_peer[d]) for d in (1, 2, 3)]
    cp.finish()
    for c in [out_q] + outs:
        c.wait()
    for c in cs:
        c.wait_recv()
    scale_ref[...] = lax.rsqrt(sq_mine[...] + sq_in[1] + sq_in[2] + sq_in[3] + norm_eps)
    cp.finish()


def last_kernel(mom_ref, grad_ref, q_ref, st_ref, scale_ref, nm_ref, nf_ref, lb_ref):
    @pl.when(pl.program_id(0) == 0)
    def _():
        lb_ref[...] = q_ref[...]

    st = st_ref[...]
    nm_ref[...] = (mom_ref[...] + grad_ref[...].astype(F32)) - (1.0 - momentum_decay) * dot(
        q_ref[...].astype(BF), st.astype(BF))
    nf_ref[...] = jnp.transpose(st) * scale_ref[0:1, :]


def body(gradient, momentum, right_factor):
    V = pltpu.VMEM
    big = pl.pallas_call(
        big_kernel,
        out_shape=(jax.ShapeDtypeStruct((R, N), F32), jax.ShapeDtypeStruct((M, R), F32),
                   jax.ShapeDtypeStruct((8, R), F32)),
        in_specs=[pl.BlockSpec(memory_space=pltpu.HBM)] * 3,
        out_specs=[pl.BlockSpec(memory_space=pl.ANY)] * 2 + [pl.BlockSpec(memory_space=V)],
        scratch_shapes=[
            V((M, N), F32), V((N, R), F32), V((M, N), BF), V((M, N), BF),
            V((N, R), BF), V((N, R), BF), V((NB, M, BK), F32), V((NB, M, BK), F32), V((2 * BK, M), BF),
            V((NB, YC // 2, BK), F32), V((NB, YC // 2, BK), F32), V((NB, YC, BK), F32), V((NB, YC, BK), F32),
            V((2 * GH, BK), F32), V((GH, BK), F32), V((16, GP, BK), F32), V((GP, BK), F32), V((4, GP, BK), F32),
            V((2 * GH, BK), F32), V((R, R), F32), V((BK, BK), F32),
            V((NB, 64, N), F32),
            V((NB, 2, 2, 8, N // 2), F32), V((NB, 2, 2, 8, N), F32), V((NB, 2, 8, N), F32),
            V((NB, 2, 4, 8, N // 4), F32), V((R, N), F32), V((R, N), F32),
            V((8, R), F32), V((4, 8, R), F32),
            pltpu.SemaphoreType.DMA((N_SEMS,)), pltpu.SemaphoreType.DMA((N_SEMS,)), pltpu.SemaphoreType.DMA((9,)), pltpu.SemaphoreType.REGULAR((3,)),
        ],
        compiler_params=pltpu.CompilerParams(
            collective_id=0, has_side_effects=True, vmem_limit_bytes=50 << 20),
        cost_estimate=pl.CostEstimate(flops=4 * M * N * R * 3, bytes_accessed=20 << 20, transcendentals=0),
    )
    st, q, scale = big(momentum, gradient, right_factor)
    tile = 512
    return pl.pallas_call(
        last_kernel,
        grid=(N // tile,),
        out_shape=(jax.ShapeDtypeStruct((M, N), F32), jax.ShapeDtypeStruct((N, R), F32),
                   jax.ShapeDtypeStruct((M, R), F32)),
        in_specs=[pl.BlockSpec((M, tile), lambda n: (0, n)), pl.BlockSpec((M, tile), lambda n: (0, n)),
                  pl.BlockSpec((M, R), lambda n: (0, 0)), pl.BlockSpec((R, tile), lambda n: (0, n)),
                  pl.BlockSpec((8, R), lambda n: (0, 0))],
        out_specs=[pl.BlockSpec((M, tile), lambda n: (0, n)), pl.BlockSpec((tile, R), lambda n: (n, 0)),
                   pl.BlockSpec((M, R), lambda n: (0, 0))],
        compiler_params=pltpu.CompilerParams(vmem_limit_bytes=24 << 20),
        cost_estimate=pl.CostEstimate(flops=2 * M * N * R, bytes_accessed=30 << 20, transcendentals=0),
    )(momentum, gradient, q, st, scale)


def solution(mesh):
    return jax.shard_map(
        body,
        mesh=mesh,
        in_specs=(P("rows", "cols"), P("rows", "cols"), P("cols", None)),
        out_specs=(P("rows", "cols"), P("cols", None), P("rows", None)),
        check_vma=False,
    )
```
